256 devices in a mesh: dp: 16 (over x, z_lo), shard: 16 (over z_hi, y, core).
Axes of the slice: x: 4, y: 4, z: 8 (z_hi: 2, z_lo: 4; z = z_hi * 4 + z_lo), core: 2. Of those that a mesh axis runs over, the one named last changes fastest.
Arguments:
- patches: bfloat16 [32768, 3072], P(('dp', 'shard')), may hold values from -16.8 to 16.8
- query_cot: bfloat16 [32768, 4096], P('dp', 'shard'), may hold values from -5.1439285 to 5.1439285
- master: float32 [3072, 4096], P('dp', 'shard'), may hold values from -3 to 3
- moment: float32 [3072, 4096], P('dp', 'shard'), may hold values from -1.2 to 1.2
- second: float32 [3072, 4096], P('dp', 'shard'), may hold values from 0.25 to 4
Outputs:
- new_weight: bfloat16 [3072, 4096], P(None, 'shard')
- new_master: float32 [3072, 4096], P('dp', 'shard')
- new_moment: float32 [3072, 4096], P('dp', 'shard')
- new_second: float32 [3072, 4096], P('dp', 'shard')
The draws below stay inside these ranges and needn't reach their ends.
All inputs are finite; a program needn't handle non-finite values.
Results may differ from the reference program's by a relative error of at most 0.007.
Values may be sent and summed in bfloat16 or wider, within the bound.
A program may use at most 192 MiB of HBM per device.

```python
import math
import jax
import jax.numpy as jnp
from jax import lax

D = 3072
HEAD = 128
QW = 4096
TOKENS = 32768
N_DP = 16


def column_scales(key, count):
    ramp = 3.0 ** (jnp.arange(count, dtype=jnp.float32) / (count - 1))
    rough = jnp.exp(jax.random.uniform(key, (count,), jnp.float32, jnp.log(0.6), jnp.log(1.6)))
    return ramp * rough


def ramped_block(key, rows, count):
    scale_key, value_key = jax.random.split(key)
    scales = column_scales(scale_key, count)
    values = jnp.clip(jax.random.normal(value_key, (rows, count), jnp.float32), -3.5, 3.5)
    return values * scales[None, :]


def draw_patches(key, part):
    key = jax.random.fold_in(key, 11)
    return ramped_block(key, TOKENS, D).astype(jnp.bfloat16)


def draw_query_cot(key, part):
    key = jax.random.fold_in(key, 23)
    factor = (D / TOKENS) ** 0.5
    return (ramped_block(key, TOKENS, QW) * factor).astype(jnp.bfloat16)


def steps_of(rng, dims, pieces, smallest, high):
    level = 1.0
    for position, parts in pieces:
        heights = jax.random.uniform(jax.random.fold_in(jax.random.fold_in(rng, 6), position), (parts,), jnp.float32, smallest / len(pieces), high / len(pieces))
        level = level * jnp.repeat(jnp.exp(heights), dims[position] // parts).reshape((-1,) + (1,) * (len(dims) - 1 - position))
    return level


def centred(stream_key, extent, scale, bound, shards=(), kind=jnp.bfloat16):
    drawn = jax.random.normal(stream_key, extent, jnp.float32) * scale
    if len(shards) > 0:
        drawn = steps_of(stream_key, extent, shards, -0.22, 0.18) * drawn
    return jnp.clip(drawn, min=-bound, max=bound).astype(kind)


def setup_inputs(seed: int = 0) -> dict:
    streams_of = jax.random.split(jax.random.key(seed), 6)
    return {
        "patches": draw_patches(jax.random.fold_in(streams_of[5], 71), 0),
        "query_cot": draw_query_cot(jax.random.fold_in(streams_of[5], 71), 0),
        "master": centred(streams_of[2], (D, QW), 0.5, 3.0, ((0, 16), (1, 16)), jnp.float32),
        "moment": centred(streams_of[3], (D, QW), 0.2, 1.2, ((0, 16), (1, 16)), jnp.float32),
        "second": jnp.clip(jnp.exp(math.log(4.0) - 2.7725887 * jax.random.uniform(streams_of[4], (D, QW), jnp.float32) ** steps_of(streams_of[4], (D, QW), ((0, 16), (1, 16)), -0.2, 0.2)), 0.25, 4.0),
    }


MOMENT_FIX = 0.9999734386011124
SECOND_FIX = 0.994079470779666

def head_backward(query, cot_block):
    rows = query.shape[0]
    grouped = query.reshape(rows, -1, HEAD)
    centre = lax.optimization_barrier(jnp.mean(grouped, axis=2, keepdims=True))
    spread = lax.optimization_barrier(jnp.mean((grouped - centre) ** 2, axis=2, keepdims=True))
    rstd = 1.0 / jnp.sqrt(spread + 1e-06)
    normed = (grouped - centre) * rstd
    upper = cot_block.astype(jnp.float32).reshape(rows, -1, HEAD)
    inner = lax.optimization_barrier(jnp.mean(upper * normed, axis=2, keepdims=True))
    dquery = rstd * (upper - lax.optimization_barrier(jnp.mean(upper, axis=2, keepdims=True)) - normed * inner)
    return dquery.reshape(rows, -1).astype(jnp.bfloat16)

def full_grad(patches, weight, query_cot):
    blocks = patches.reshape(N_DP, -1, D)
    cots = query_cot.reshape(N_DP, -1, QW)

    def step(total, pair):
        rows_block, cot_block = pair
        query = jnp.dot(rows_block, weight, preferred_element_type=jnp.float32)
        dquery = head_backward(query, cot_block)
        term = lax.dot_general(rows_block, dquery, (((0,), (0,)), ((), ())), preferred_element_type=jnp.float32)
        return (total + term, None)
    total, _ = lax.scan(step, jnp.zeros((D, QW), jnp.float32), (blocks, cots))
    return total

def reference(patches, query_cot, master, moment, second):
    weight0 = master.astype(jnp.bfloat16)
    grad1 = full_grad(patches, weight0, query_cot)
    total = jnp.sum(grad1 * grad1)
    scale = jnp.sqrt(jnp.float32(D * QW)) / jnp.sqrt(total + 1e-12)
    weight1 = (weight0.astype(jnp.float32) + scale * grad1).astype(jnp.bfloat16)
    grad2 = full_grad(patches, weight1, query_cot)
    new_moment = 0.9 * moment + 0.1 * grad2
    new_second = 0.95 * second + 0.05 * grad2 * grad2
    update = new_moment / MOMENT_FIX / (jnp.sqrt(new_second / SECOND_FIX) + 1e-08) + 0.1 * master
    new_master = master - 0.05 * update
    return (new_master.astype(jnp.bfloat16), new_master, new_moment, new_second)
```

```python
import jax
import jax.numpy as jnp
from jax import lax
from jax.experimental import pallas as pl
from jax.experimental.pallas import tpu as pltpu
from jax.sharding import PartitionSpec as P

D = 3072
HEAD = 128
QW = 4096
COLS = 256
REPLICA = 2048
BLOCK = 128
PART = 192
HALF = 96
PIECE = 768

MOMENT_FIX = 0.9999734386011124
SECOND_FIX = 0.994079470779666

MESH = pl.DeviceIdType.MESH
f32 = jnp.float32
bf16 = jnp.bfloat16


class Slots:
    def __init__(self):
        self.count = 0

    def take(self, *dims):
        start, size = self.count, 1
        for dim in dims:
            size *= dim
        self.count += size

        def at(*index):
            flat = 0
            for dim, i in zip(dims, index, strict=True):
                flat = flat * dim + i
            return start + flat

        return at


SLOTS = Slots()
Y_SEM = SLOTS.take(2, 2, 4)
YF_SEM = SLOTS.take(2, 2, 4)
Z4_SEM = SLOTS.take(4)
SIB_SEM = SLOTS.take(2, 7)
AG_Z, AG_X, AG_F = SLOTS.take(3, 4), SLOTS.take(3, 2, 4), SLOTS.take(3, 2, 4)
RS_F, RS_X, RS_Z = SLOTS.take(2, 2, 4), SLOTS.take(2, 2, 4), SLOTS.take(2, 4)
SUM_SEM = SLOTS.take(2, 16)
N_SEM = SLOTS.count


def norm_backward(query, centred_cot):
    parts = []
    for head in range(COLS // HEAD):
        lanes = slice(head * HEAD, (head + 1) * HEAD)
        x, c = query[:, lanes], centred_cot[:, lanes]
        x = x - jnp.sum(x, axis=1, keepdims=True) * (1.0 / HEAD)
        var = jnp.sum(x * x, axis=1, keepdims=True) * (1.0 / HEAD)
        rstd = 1.0 / jnp.sqrt(var + 1e-06)
        normed = x * rstd
        inner = jnp.sum(c * normed, axis=1, keepdims=True) * (1.0 / HEAD)
        parts.append((rstd * (c - normed * inner)).astype(bf16))
    return jnp.concatenate(parts, axis=1)


def kernel(
    patches, cot, master, moment, second,
    new_weight, new_master, new_moment, new_second,
    pat, cots, centred, w0, g1, w1, nw, dq,
    plus, minus, mine, b_two, b_plus, b_minus, b_z, r_f, r_x, r_z, sums, tile,
    ssem, rsem, lsem,
):
    dp, sh = lax.axis_index("dp"), lax.axis_index("shard")
    x, zl = dp // 4, dp % 4
    y = (sh // 2) % 4

    def at_x(step):
        return ((x + step) % 4) * 4 + zl, sh

    def at_z(step):
        return x * 4 + (zl + step) % 4, sh

    def at_y(step):
        return dp, (sh // 8) * 8 + ((y + step) % 4) * 2 + sh % 2

    far = (dp, (sh + 8) % 16)
    sibling = (dp, sh + 1 - 2 * (sh % 2))

    def copy(src, dst, slot, to):
        return pltpu.make_async_remote_copy(
            src_ref=src, dst_ref=dst, send_sem=ssem.at[slot], recv_sem=rsem.at[slot],
            device_id=to, device_id_type=MESH,
        )

    started = []

    def send(src, dst, slot, to):
        one = copy(src, dst, slot, to)
        one.start()
        started.append(one)

    def arrived(ref, slot):
        copy(ref, ref, slot, sibling).wait_recv()

    def rows(start, size, by):
        return pl.ds(pl.multiple_of(start, by), size)

    own = pat.at[rows(sh * BLOCK, BLOCK, BLOCK)]
    load = pltpu.make_async_copy(patches, own, lsem.at[0])
    load.start()
    load_cot = pltpu.make_async_copy(cot, cots, lsem.at[1])
    load_cot.start()
    barrier = pltpu.get_barrier_semaphore()

    @pl.loop(1, 16)
    def _(p):
        pl.semaphore_signal(barrier, inc=1, device_id=((dp + p) % 16, sh), device_id_type=MESH)
        pl.semaphore_signal(barrier, inc=1, device_id=(dp, (sh + p) % 16), device_id_type=MESH)

    w0[rows(dp * PART, PART, PART), :] = master[...].astype(bf16)
    load.wait()
    with jax.named_scope("entry"):
        pl.semaphore_wait(barrier, 30)

    def gather_start(k, buf):
        part = buf.at[rows(dp * PART, PART, PART)]
        for r in (1, 3, 2):
            send(part, part, AG_Z(k, r), at_z(r))
        send(part, part, AG_X(k, 0, 0), at_x(1))
        send(part, part, AG_X(k, 1, 0), at_x(3))

    def gather_z(k, buf):
        for r in (1, 3, 2):
            part = buf.at[rows((x * 4 + (zl + 4 - r) % 4) * PART, PART, PART)]
            arrived(part, AG_Z(k, r))
            send(part, part, AG_X(k, 0, r), at_x(1))
            send(part, part, AG_X(k, 1, r), at_x(3))

    def gather_x(k, buf):
        for r in (0, 1, 3, 2):
            zz = (zl + 4 - r) % 4
            low = ((x + 3) % 4 * 4 + zz) * PART
            arrived(buf.at[rows(low, PART, PART)], AG_X(k, 0, r))
            half = buf.at[rows(low, HALF, HALF)]
            send(half, half, AG_F(k, 0, r), at_x(1))
            high = ((x + 1) % 4 * 4 + zz) * PART
            arrived(buf.at[rows(high, PART, PART)], AG_X(k, 1, r))
            half = buf.at[rows(high + HALF, HALF, HALF)]
            send(half, half, AG_F(k, 1, r), at_x(3))

    def gather_end(k, buf):
        for r in (0, 1, 3, 2):
            start = ((x + 2) % 4 * 4 + (zl + 4 - r) % 4) * PART
            arrived(buf.at[rows(start, HALF, HALF)], AG_F(k, 0, r))
            arrived(buf.at[rows(start + HALF, HALF, HALF)], AG_F(k, 1, r))

    def home(half):
        return (sh + 8 * half) % 16

    def y_block(half, step):
        base = home(half)
        return ((base // 8) * 8 + ((y + step) % 4) * 2 + base % 2) * BLOCK

    def y_send(half, q):
        part = pat.at[rows(home(half) * BLOCK + q * 32, 32, 32)]
        send(part, part, Y_SEM(half, 0, q), at_y(1))
        send(part, part, Y_SEM(half, 1, q), at_y(3))

    def y_forward(half, q):
        low = y_block(half, 3) + q * 32
        arrived(pat.at[rows(low, 32, 32)], Y_SEM(half, 0, q))
        part = pat.at[rows(low, 16, 16)]
        send(part, part, YF_SEM(half, 0, q), at_y(1))
        high = y_block(half, 1) + q * 32
        arrived(pat.at[rows(high, 32, 32)], Y_SEM(half, 1, q))
        part = pat.at[rows(high + 16, 16, 16)]
        send(part, part, YF_SEM(half, 1, q), at_y(3))

    def y_last(half, q):
        start = y_block(half, 2) + q * 32
        arrived(pat.at[rows(start, 16, 16)], YF_SEM(half, 0, q))
        arrived(pat.at[rows(start + 16, 16, 16)], YF_SEM(half, 1, q))
        part = pat.at[rows(start, 32, 32)]
        send(part, part, SIB_SEM(half, 3 + q), sibling)

    def share(half, step, slot):
        part = pat.at[rows(y_block(half, step), BLOCK, BLOCK)]
        send(part, part, SIB_SEM(half, slot), sibling)

    def theirs(half, step):
        return y_block(half, step) // (2 * BLOCK) * (2 * BLOCK) + (1 - sh % 2) * BLOCK

    def shared(half, step, slot):
        arrived(pat.at[rows(theirs(half, step), BLOCK, BLOCK)], SIB_SEM(half, slot))

    def shared_last(half):
        for q in range(4):
            arrived(pat.at[rows(theirs(half, 2) + q * 32, 32, 32)], SIB_SEM(half, 3 + q))

    def block_of(half, step):
        part = rows(y_block(half, step) // (2 * BLOCK) * (2 * BLOCK), 2 * BLOCK, 2 * BLOCK)
        query = jnp.dot(pat[part, :], w0[...], preferred_element_type=f32)
        dq[part, :] = norm_backward(query, centred[part, :])

    for q in range(4):
        y_send(0, q)
    for q in range(4):
        part = pat.at[rows(sh * BLOCK + q * 32, 32, 32)]
        send(part, part, Z4_SEM(q), far)
    share(0, 0, 0)
    gather_start(0, w0)

    load_cot.wait()

    @pl.loop(0, 8)
    def _(i):
        part = rows(i * 256, 256, 256)
        for head in range(COLS // HEAD):
            lanes = slice(head * HEAD, (head + 1) * HEAD)
            c = cots[part, lanes].astype(f32)
            centred[part, lanes] = c - jnp.sum(c, axis=1, keepdims=True) * (1.0 / HEAD)

    def z4_pass(q):
        arrived(pat.at[rows(home(1) * BLOCK + q * 32, 32, 32)], Z4_SEM(q))
        y_send(1, q)

    with jax.named_scope("w0_z"):
        gather_z(0, w0)
    with jax.named_scope("y0"):
        for q in range(4):
            y_forward(0, q)
    share(0, 3, 1)
    share(0, 1, 2)
    with jax.named_scope("w0_x"):
        gather_x(0, w0)
        gather_end(0, w0)
    with jax.named_scope("z4a"):
        z4_pass(0)
        z4_pass(1)
    shared(0, 0, 0)
    block_of(0, 0)
    shared(0, 3, 1)
    block_of(0, 3)
    shared(0, 1, 2)
    block_of(0, 1)
    with jax.named_scope("y0_last"):
        for q in range(4):
            y_last(0, q)
    with jax.named_scope("z4b"):
        z4_pass(2)
        z4_pass(3)
    share(1, 0, 0)
    shared_last(0)
    block_of(0, 2)
    shared(1, 0, 0)
    block_of(1, 0)
    with jax.named_scope("y1"):
        for q in range(4):
            y_forward(1, q)
    share(1, 3, 1)
    share(1, 1, 2)
    with jax.named_scope("blocks"):
        shared(1, 3, 1)
        block_of(1, 3)
        shared(1, 1, 2)
        block_of(1, 1)
    with jax.named_scope("y1_last"):
        for q in range(4):
            y_last(1, q)
    shared_last(1)
    block_of(1, 2)

    def piece(step):
        lanes = pl.ds(pl.multiple_of((x + step) % 4 * PIECE, PIECE), PIECE)
        return lax.dot_general(
            pat[:, lanes], dq[...], (((0,), (0,)), ((), ())), preferred_element_type=f32
        )

    ORDER = (2, 1, 3, 0)

    def reduce_scatter(k):
        with jax.named_scope("rs_two"):
            b_two[...] = piece(2).astype(bf16)
        for r in ORDER:
            start = (zl + r) % 4 * PART
            send(b_two.at[rows(start, HALF, HALF)], r_f.at[k, 0, r], RS_F(k, 0, r), at_x(1))
            send(b_two.at[rows(start + HALF, HALF, HALF)], r_f.at[k, 1, r], RS_F(k, 1, r), at_x(3))
        with jax.named_scope("rs_pm"):
            plus[...] = piece(1)
            minus[...] = piece(3)
        with jax.named_scope("rs_x"):
            for r in ORDER:
                start = (zl + r) % 4 * PART
                low, high = rows(start, HALF, HALF), rows(start + HALF, HALF, HALF)
                both = rows(start, PART, PART)
                arrived(r_f.at[k, 0, r], RS_F(k, 0, r))
                b_plus[low, :] = (plus[low, :] + r_f[k, 0, r].astype(f32)).astype(bf16)
                b_plus[high, :] = plus[high, :].astype(bf16)
                send(b_plus.at[both], r_x.at[k, 0, r], RS_X(k, 0, r), at_x(1))
                arrived(r_f.at[k, 1, r], RS_F(k, 1, r))
                b_minus[low, :] = minus[low, :].astype(bf16)
                b_minus[high, :] = (minus[high, :] + r_f[k, 1, r].astype(f32)).astype(bf16)
                send(b_minus.at[both], r_x.at[k, 1, r], RS_X(k, 1, r), at_x(3))
                if r == ORDER[0]:
                    mine[...] = piece(0)
        with jax.named_scope("rs_z"):
            for r in ORDER:
                both = rows((zl + r) % 4 * PART, PART, PART)
                arrived(r_x.at[k, 0, r], RS_X(k, 0, r))
                arrived(r_x.at[k, 1, r], RS_X(k, 1, r))
                total = mine[both, :] + r_x[k, 0, r].astype(f32) + r_x[k, 1, r].astype(f32)
                if r:
                    b_z[k, r] = total.astype(bf16)
                    send(b_z.at[k, r], r_z.at[k, r], RS_Z(k, r), at_z(r))
        with jax.named_scope("rs_end"):
            for r in (2, 1, 3):
                arrived(r_z.at[k, r], RS_Z(k, r))
                total = total + r_z[k, r].astype(f32)
        return total

    def finish():
        for one in started:
            one.wait_send()
        started.clear()

    grad1 = reduce_scatter(0)
    finish()
    g1[rows(dp * PART, PART, PART), :] = grad1.astype(bf16)
    gather_start(1, g1)

    square = (grad1 * grad1).reshape(PART // 8, 8, COLS)
    square = jnp.sum(square, axis=0)
    tile[0] = square[:, :128] + square[:, 128:]

    def sum_copy(stage, p):
        to = ((dp + p) % 16, sh) if stage == 0 else (dp, (sh + p) % 16)
        return copy(tile.at[stage], sums.at[stage, p], SUM_SEM(stage, p), to)

    def sum_start(stage):
        @pl.loop(1, 16)
        def _(p):
            sum_copy(stage, p).start()

    def sum_end(stage):
        def add(p, total):
            sum_copy(stage, p).wait()
            return total + sums[stage, p]

        return lax.fori_loop(1, 16, add, tile[stage])

    sum_start(0)
    with jax.named_scope("g1_z"):
        gather_z(1, g1)
    with jax.named_scope("sum0"):
        tile[1] = sum_end(0)
    sum_start(1)
    with jax.named_scope("g1_x"):
        gather_x(1, g1)
    with jax.named_scope("sum1"):
        total = jnp.sum(sum_end(1))
    scale = jnp.sqrt(f32(D * QW)) / jnp.sqrt(total + 1e-12)
    with jax.named_scope("g1_end"):
        gather_end(1, g1)

    with jax.named_scope("pass2"):

        @pl.loop(0, 8)
        def _(i):
            part = rows(i * 384, 384, 384)
            w1[part, :] = (w0[part, :].astype(f32) + scale * g1[part, :].astype(f32)).astype(bf16)

        @pl.loop(0, 4)
        def _(i):
            part = rows(i * 512, 512, 512)
            query = jnp.dot(pat[part, :], w1[...], preferred_element_type=f32)
            dq[part, :] = norm_backward(query, centred[part, :])

    finish()
    grad2 = reduce_scatter(1)
    finish()
    weights = master[...]
    next_moment = 0.9 * moment[...] + 0.1 * grad2
    next_second = 0.95 * second[...] + 0.05 * grad2 * grad2
    update = next_moment / MOMENT_FIX / (jnp.sqrt(next_second / SECOND_FIX) + 1e-08) + 0.1 * weights
    next_master = weights - 0.05 * update
    nw[rows(dp * PART, PART, PART), :] = next_master.astype(bf16)
    gather_start(2, nw)
    new_master[...] = next_master
    new_moment[...] = next_moment
    new_second[...] = next_second
    with jax.named_scope("nw"):
        gather_z(2, nw)
        gather_x(2, nw)
        gather_end(2, nw)
    out = pltpu.make_async_copy(nw, new_weight, lsem.at[0])
    out.start()
    finish()
    out.wait()


def on_device(patches, cot, master, moment, second):
    state = jax.ShapeDtypeStruct((PART, COLS), f32)
    any_ref, vmem = pl.BlockSpec(memory_space=pl.ANY), pl.BlockSpec(memory_space=pltpu.VMEM)
    return pl.pallas_call(
        kernel,
        name="sam_step",
        out_shape=(jax.ShapeDtypeStruct((D, COLS), bf16), state, state, state),
        in_specs=[any_ref, any_ref, vmem, vmem, vmem],
        out_specs=(any_ref, vmem, vmem, vmem),
        scratch_shapes=[
            pltpu.VMEM((REPLICA, D), bf16),
            pltpu.VMEM((REPLICA, COLS), bf16),
            pltpu.VMEM((REPLICA, COLS), f32),
            pltpu.VMEM((D, COLS), bf16),
            pltpu.VMEM((D, COLS), bf16),
            pltpu.VMEM((D, COLS), bf16),
            pltpu.VMEM((D, COLS), bf16),
            pltpu.VMEM((REPLICA, COLS), bf16),
            pltpu.VMEM((PIECE, COLS), f32),
            pltpu.VMEM((PIECE, COLS), f32),
            pltpu.VMEM((PIECE, COLS), f32),
            pltpu.VMEM((PIECE, COLS), bf16),
            pltpu.VMEM((PIECE, COLS), bf16),
            pltpu.VMEM((PIECE, COLS), bf16),
            pltpu.VMEM((2, 4, PART, COLS), bf16),
            pltpu.VMEM((2, 2, 4, HALF, COLS), bf16),
            pltpu.VMEM((2, 2, 4, PART, COLS), bf16),
            pltpu.VMEM((2, 4, PART, COLS), bf16),
            pltpu.VMEM((2, 16, 8, 128), f32),
            pltpu.VMEM((2, 8, 128), f32),
            pltpu.SemaphoreType.DMA((N_SEM,)),
            pltpu.SemaphoreType.DMA((N_SEM,)),
            pltpu.SemaphoreType.DMA((2,)),
        ],
        compiler_params=pltpu.CompilerParams(
            collective_id=0, has_side_effects=True, vmem_limit_bytes=56 * 2**20
        ),
    )(patches, cot, master, moment, second)


def solution(mesh):
    in_specs = (
        P(("dp", "shard"), None),
        P("dp", "shard"),
        P("dp", "shard"),
        P("dp", "shard"),
        P("dp", "shard"),
    )
    out_specs = (P(None, "shard"), P("dp", "shard"), P("dp", "shard"), P("dp", "shard"))
    return jax.shard_map(
        on_device, mesh=mesh, in_specs=in_specs, out_specs=out_specs, check_vma=False
    )
```

```python
import jax
import jax.numpy as jnp
from jax import lax
from jax.experimental import pallas as pl
from jax.experimental.pallas import tpu as pltpu
from jax.sharding import PartitionSpec as P

D = 3072
HEAD = 128
QW = 4096
COLS = 256
REPLICA = 2048
BLOCK = 128
PART = 192
PIECE = 768
CUTS = 2
SUB = PART // CUTS
HALF = SUB // 2

MOMENT_FIX = 0.9999734386011124
SECOND_FIX = 0.994079470779666

MESH = pl.DeviceIdType.MESH
f32 = jnp.float32
bf16 = jnp.bfloat16


class Slots:
    def __init__(self):
        self.count = 0

    def take(self, *dims):
        start, size = self.count, 1
        for dim in dims:
            size *= dim
        self.count += size

        def at(*index):
            flat = 0
            for dim, i in zip(dims, index, strict=True):
                flat = flat * dim + i
            return start + flat

        return at


SLOTS = Slots()
Y_SEM = SLOTS.take(2, 2, 4)
YF_SEM = SLOTS.take(2, 2, 4)
Z4_SEM = SLOTS.take(4)
SIB_SEM = SLOTS.take(2, 7)
AG_Z, AG_X, AG_F = SLOTS.take(3, CUTS, 4), SLOTS.take(3, CUTS, 2, 4), SLOTS.take(3, CUTS, 2, 4)
RS_F, RS_X, RS_Z = SLOTS.take(2, CUTS, 2, 4), SLOTS.take(2, CUTS, 2, 4), SLOTS.take(2, CUTS, 4)
SUM_SEM = SLOTS.take(2, 16)
N_SEM = SLOTS.count


def norm_backward(query, centred_cot):
    parts = []
    for head in range(COLS // HEAD):
        lanes = slice(head * HEAD, (head + 1) * HEAD)
        x, c = query[:, lanes], centred_cot[:, lanes]
        x = x - jnp.sum(x, axis=1, keepdims=True) * (1.0 / HEAD)
        var = jnp.sum(x * x, axis=1, keepdims=True) * (1.0 / HEAD)
        rstd = 1.0 / jnp.sqrt(var + 1e-06)
        normed = x * rstd
        inner = jnp.sum(c * normed, axis=1, keepdims=True) * (1.0 / HEAD)
        parts.append((rstd * (c - normed * inner)).astype(bf16))
    return jnp.concatenate(parts, axis=1)


def kernel(
    patches, cot, master_in, moment_in, second_in,
    new_weight, new_master, new_moment, new_second,
    master, moment, second, pat, cots, centred, w0, g1, w1, nw, dq,
    plus, minus, mine, b_two, b_plus, b_minus, b_z, r_f, r_x, r_z, sums, tile, query,
    ssem, rsem, lsem,
):
    dp, sh = lax.axis_index("dp"), lax.axis_index("shard")
    x, zl = dp // 4, dp % 4
    y = (sh // 2) % 4

    def at_x(step):
        return ((x + step) % 4) * 4 + zl, sh

    def at_z(step):
        return x * 4 + (zl + step) % 4, sh

    def at_y(step):
        return dp, (sh // 8) * 8 + ((y + step) % 4) * 2 + sh % 2

    far = (dp, (sh + 8) % 16)
    sibling = (dp, sh + 1 - 2 * (sh % 2))

    def copy(src, dst, slot, to):
        return pltpu.make_async_remote_copy(
            src_ref=src, dst_ref=dst, send_sem=ssem.at[slot], recv_sem=rsem.at[slot],
            device_id=to, device_id_type=MESH,
        )

    started = []

    def send(src, dst, slot, to):
        one = copy(src, dst, slot, to)
        one.start()
        started.append(one)

    def finish():
        for one in started:
            one.wait_send()
        started.clear()

    def arrived(ref, slot):
        copy(ref, ref, slot, sibling).wait_recv()

    def rows(start, size, by):
        return pl.ds(pl.multiple_of(start, by), size)

    barrier = pltpu.get_barrier_semaphore()

    @pl.loop(1, 16)
    def _(p):
        pl.semaphore_signal(barrier, inc=1, device_id=(dp, (sh + p) % 16), device_id_type=MESH)
        pl.semaphore_signal(barrier, inc=1, device_id=((dp + p) % 16, sh), device_id_type=MESH)

    own = pat.at[rows(sh * BLOCK, BLOCK, BLOCK)]
    loads = [
        pltpu.make_async_copy(src, dst, lsem.at[i])
        for i, (src, dst) in enumerate(
            ((master_in, master), (patches, own), (cot, cots), (moment_in, moment), (second_in, second))
        )
    ]
    for load in loads:
        load.start()
    loads[0].wait()
    w0[rows(dp * PART, PART, PART), :] = master[...].astype(bf16)
    loads[1].wait()
    with jax.named_scope("entry"):
        pl.semaphore_wait(barrier, 30)

    def gather_start(k, buf, h):
        part = buf.at[rows(dp * PART + h * SUB, SUB, SUB)]
        for r in (2, 1, 3):
            send(part, part, AG_Z(k, h, r), at_z(r))
        send(part, part, AG_X(k, h, 0, 0), at_x(1))
        send(part, part, AG_X(k, h, 1, 0), at_x(3))

    def gather_z(k, buf, h):
        for r in (1, 3, 2):
            part = buf.at[rows((x * 4 + (zl + 4 - r) % 4) * PART + h * SUB, SUB, SUB)]
            arrived(part, AG_Z(k, h, r))
            send(part, part, AG_X(k, h, 0, r), at_x(1))
            send(part, part, AG_X(k, h, 1, r), at_x(3))

    def gather_x(k, buf, h):
        for r in (0, 1, 3, 2):
            zz = (zl + 4 - r) % 4
            low = ((x + 3) % 4 * 4 + zz) * PART + h * SUB
            arrived(buf.at[rows(low, SUB, SUB)], AG_X(k, h, 0, r))
            half = buf.at[rows(low, HALF, HALF)]
            send(half, half, AG_F(k, h, 0, r), at_x(1))
            high = ((x + 1) % 4 * 4 + zz) * PART + h * SUB
            arrived(buf.at[rows(high, SUB, SUB)], AG_X(k, h, 1, r))
            half = buf.at[rows(high + HALF, HALF, HALF)]
            send(half, half, AG_F(k, h, 1, r), at_x(3))

    def gather_end(k, buf, h):
        for r in (0, 1, 3, 2):
            start = ((x + 2) % 4 * 4 + (zl + 4 - r) % 4) * PART + h * SUB
            arrived(buf.at[rows(start, HALF, HALF)], AG_F(k, h, 0, r))
            arrived(buf.at[rows(start + HALF, HALF, HALF)], AG_F(k, h, 1, r))

    def home(half):
        return (sh + 8 * half) % 16

    def y_block(half, step):
        base = home(half)
        return ((base // 8) * 8 + ((y + step) % 4) * 2 + base % 2) * BLOCK

    def y_send(half, q):
        part = pat.at[rows(home(half) * BLOCK + q * 32, 32, 32)]
        send(part, part, Y_SEM(half, 0, q), at_y(1))
        send(part, part, Y_SEM(half, 1, q), at_y(3))

    def y_forward(half, q):
        low = y_block(half, 3) + q * 32
        arrived(pat.at[rows(low, 32, 32)], Y_SEM(half, 0, q))
        part = pat.at[rows(low, 16, 16)]
        send(part, part, YF_SEM(half, 0, q), at_y(1))
        high = y_block(half, 1) + q * 32
        arrived(pat.at[rows(high, 32, 32)], Y_SEM(half, 1, q))
        part = pat.at[rows(high + 16, 16, 16)]
        send(part, part, YF_SEM(half, 1, q), at_y(3))

    def y_last(half, q):
        start = y_block(half, 2) + q * 32
        arrived(pat.at[rows(start, 16, 16)], YF_SEM(half, 0, q))
        arrived(pat.at[rows(start + 16, 16, 16)], YF_SEM(half, 1, q))
        part = pat.at[rows(start, 32, 32)]
        send(part, part, SIB_SEM(half, 3 + q), sibling)

    def share(half, step, slot):
        part = pat.at[rows(y_block(half, step), BLOCK, BLOCK)]
        send(part, part, SIB_SEM(half, slot), sibling)

    def theirs(half, step):
        return y_block(half, step) // (2 * BLOCK) * (2 * BLOCK) + (1 - sh % 2) * BLOCK

    def shared(half, step, slot):
        arrived(pat.at[rows(theirs(half, step), BLOCK, BLOCK)], SIB_SEM(half, slot))

    def shared_last(half):
        for q in range(4):
            arrived(pat.at[rows(theirs(half, 2) + q * 32, 32, 32)], SIB_SEM(half, 3 + q))

    def block_of(half, step):
        part = rows(y_block(half, step) // (2 * BLOCK) * (2 * BLOCK), 2 * BLOCK, 2 * BLOCK)
        query = jnp.dot(pat[part, :], w0[...], preferred_element_type=f32)
        dq[part, :] = norm_backward(query, centred[part, :])

    for h in range(CUTS):
        gather_start(0, w0, h)
    for q in range(4):
        y_send(0, q)
    share(0, 0, 0)

    loads[2].wait()

    @pl.loop(0, 8)
    def _(i):
        part = rows(i * 256, 256, 256)
        for head in range(COLS // HEAD):
            lanes = slice(head * HEAD, (head + 1) * HEAD)
            c = cots[part, lanes].astype(f32)
            centred[part, lanes] = c - jnp.sum(c, axis=1, keepdims=True) * (1.0 / HEAD)

    def z4_pass(q):
        arrived(pat.at[rows(home(1) * BLOCK + q * 32, 32, 32)], Z4_SEM(q))
        y_send(1, q)

    y_forward(0, 0)
    for h in range(CUTS):
        gather_z(0, w0, h)
    for q in range(4):
        part = pat.at[rows(sh * BLOCK + q * 32, 32, 32)]
        send(part, part, Z4_SEM(q), far)
    y_forward(0, 1)
    y_forward(0, 2)
    y_forward(0, 3)
    share(0, 3, 1)
    share(0, 1, 2)
    for h in range(CUTS):
        gather_x(0, w0, h)
    z4_pass(0)
    for h in range(CUTS):
        gather_end(0, w0, h)
    shared(0, 0, 0)
    block_of(0, 0)
    shared(0, 3, 1)
    block_of(0, 3)
    shared(0, 1, 2)
    block_of(0, 1)
    for q in range(4):
        y_last(0, q)
    z4_pass(1)
    shared_last(0)
    block_of(0, 2)
    y_forward(1, 0)
    z4_pass(2)
    y_forward(1, 1)
    z4_pass(3)
    share(1, 0, 0)
    y_forward(1, 2)
    shared(1, 0, 0)
    block_of(1, 0)
    y_forward(1, 3)
    share(1, 3, 1)
    share(1, 1, 2)
    for q in range(3):
        y_last(1, q)
    shared(1, 3, 1)
    block_of(1, 3)
    shared(1, 1, 2)
    block_of(1, 1)
    y_last(1, 3)
    shared_last(1)
    block_of(1, 2)

    def piece(step):
        lanes = pl.ds(pl.multiple_of((x + step) % 4 * PIECE, PIECE), PIECE)
        return lax.dot_general(
            pat[:, lanes], dq[...], (((0,), (0,)), ((), ())), preferred_element_type=f32
        )

    ORDER = (2, 1, 3, 0)

    def scatter_two(k, h):
        for r in ORDER:
            start = (zl + r) % 4 * PART + h * SUB
            send(b_two.at[rows(start, HALF, HALF)], r_f.at[k, h, 0, r], RS_F(k, h, 0, r), at_x(1))
            send(b_two.at[rows(start + HALF, HALF, HALF)], r_f.at[k, h, 1, r], RS_F(k, h, 1, r), at_x(3))

    def scatter_x(k, h):
        for r in ORDER:
            start = (zl + r) % 4 * PART + h * SUB
            low, high = rows(start, HALF, HALF), rows(start + HALF, HALF, HALF)
            both = rows(start, SUB, SUB)
            arrived(r_f.at[k, h, 0, r], RS_F(k, h, 0, r))
            b_plus[low, :] = (plus[low, :] + r_f[k, h, 0, r].astype(f32)).astype(bf16)
            b_plus[high, :] = plus[high, :].astype(bf16)
            send(b_plus.at[both], r_x.at[k, h, 0, r], RS_X(k, h, 0, r), at_x(1))
            arrived(r_f.at[k, h, 1, r], RS_F(k, h, 1, r))
            b_minus[low, :] = minus[low, :].astype(bf16)
            b_minus[high, :] = (minus[high, :] + r_f[k, h, 1, r].astype(f32)).astype(bf16)
            send(b_minus.at[both], r_x.at[k, h, 1, r], RS_X(k, h, 1, r), at_x(3))

    def scatter_z(k, h):
        for r in ORDER:
            both = rows((zl + r) % 4 * PART + h * SUB, SUB, SUB)
            arrived(r_x.at[k, h, 0, r], RS_X(k, h, 0, r))
            arrived(r_x.at[k, h, 1, r], RS_X(k, h, 1, r))
            total = mine[both, :] + r_x[k, h, 0, r].astype(f32) + r_x[k, h, 1, r].astype(f32)
            if r:
                b_z[k, h, r] = total.astype(bf16)
                send(b_z.at[k, h, r], r_z.at[k, h, r], RS_Z(k, h, r), at_z(r))
        mine[rows(zl * PART + h * SUB, SUB, SUB), :] = total

    def scatter_end(k, h):
        total = mine[rows(zl * PART + h * SUB, SUB, SUB), :]
        for r in (2, 1, 3):
            arrived(r_z.at[k, h, r], RS_Z(k, h, r))
            total = total + r_z[k, h, r].astype(f32)
        return total

    def scatter_start(k):
        b_two[...] = piece(2).astype(bf16)
        for h in range(CUTS):
            scatter_two(k, h)
        plus[...] = piece(1)
        minus[...] = piece(3)
        scatter_x(k, 0)
        mine[...] = piece(0)
        for h in range(1, CUTS):
            scatter_x(k, h)

    def squares(part):
        part = jnp.sum((part * part).reshape(SUB // 8, 8, COLS), axis=0)
        return part[:, :128] + part[:, 128:]

    scatter_start(0)
    square = None
    for h in range(CUTS):
        scatter_z(0, h)
        if h:
            gather_z(1, g1, h - 1)
        grad1 = scatter_end(0, h)
        g1[rows(dp * PART + h * SUB, SUB, SUB), :] = grad1.astype(bf16)
        gather_start(1, g1, h)
        square = squares(grad1) if square is None else square + squares(grad1)

    tile[0] = square

    def sum_copy(stage, p):
        to = ((dp + p) % 16, sh) if stage == 0 else (dp, (sh + p) % 16)
        return copy(tile.at[stage], sums.at[stage, p], SUM_SEM(stage, p), to)

    def sum_start(stage):
        @pl.loop(1, 16)
        def _(p):
            sum_copy(stage, p).start()

    def sum_end(stage):
        def add(p, total):
            sum_copy(stage, p).wait()
            return total + sums[stage, p]

        return lax.fori_loop(1, 16, add, tile[stage])

    earlier = list(started)
    started.clear()
    sum_start(0)
    for h in range(CUTS - 1):
        gather_x(1, g1, h)
    gather_z(1, g1, CUTS - 1)
    tile[1] = sum_end(0)
    sum_start(1)
    gather_x(1, g1, CUTS - 1)
    for one in earlier:
        one.wait_send()
    total = jnp.sum(sum_end(1))
    scale = jnp.sqrt(f32(D * QW)) / jnp.sqrt(total + 1e-12)

    def depth(step):
        return (x + step) % 4 * PIECE

    def tilt(step):
        part = rows(depth(step), PIECE, PIECE)
        w1[part, :] = (w0[part, :].astype(f32) + scale * g1[part, :].astype(f32)).astype(bf16)

    def share_of(part, step):
        span = rows(depth(step), PIECE, PIECE)
        return jnp.dot(pat[part, span], w1[span, :], preferred_element_type=f32)

    for step in (0, 1, 3):
        tilt(step)

    @pl.loop(0, 4)
    def _(i):
        part = rows(i * 512, 512, 512)
        query[part, :] = share_of(part, 0) + share_of(part, 1) + share_of(part, 3)

    for h in range(CUTS):
        gather_end(1, g1, h)
    tilt(2)

    @pl.loop(0, 4)
    def _(i):
        part = rows(i * 512, 512, 512)
        dq[part, :] = norm_backward(query[part, :] + share_of(part, 2), centred[part, :])


    scatter_start(1)
    for load in loads[3:]:
        load.wait()
    for h in range(CUTS):
        part = pl.ds(h * SUB, SUB)
        scatter_z(1, h)
        if h:
            gather_z(2, nw, h - 1)
        grad2 = scatter_end(1, h)
        weights = master[part, :]
        next_moment = 0.9 * moment[part, :] + 0.1 * grad2
        next_second = 0.95 * second[part, :] + 0.05 * grad2 * grad2
        update = next_moment / MOMENT_FIX / (jnp.sqrt(next_second / SECOND_FIX) + 1e-08) + 0.1 * weights
        next_master = weights - 0.05 * update
        nw[rows(dp * PART + h * SUB, SUB, SUB), :] = next_master.astype(bf16)
        gather_start(2, nw, h)
        new_master[part, :] = next_master
        new_moment[part, :] = next_moment
        new_second[part, :] = next_second
    for h in range(CUTS - 1):
        gather_x(2, nw, h)
    gather_z(2, nw, CUTS - 1)
    gather_x(2, nw, CUTS - 1)

    def place(step):
        part = rows(depth(step), PIECE, PIECE)
        new_weight[part, :] = nw[part, :]

    for step in (0, 1, 3):
        place(step)
    for h in range(CUTS):
        gather_end(2, nw, h)
    place(2)
    finish()


def on_device(patches, cot, master, moment, second):
    state = pltpu.VMEM((PART, COLS), f32)
    any_ref, vmem = pl.BlockSpec(memory_space=pl.ANY), pl.BlockSpec(memory_space=pltpu.VMEM)
    return pl.pallas_call(
        kernel,
        name="sam_step",
        out_shape=(pltpu.VMEM((D, COLS), bf16), state, state, state),
        in_specs=[any_ref] * 5,
        out_specs=(vmem, vmem, vmem, vmem),
        scratch_shapes=[
            pltpu.VMEM((PART, COLS), f32),
            pltpu.VMEM((PART, COLS), f32),
            pltpu.VMEM((PART, COLS), f32),
            pltpu.VMEM((REPLICA, D), bf16),
            pltpu.VMEM((REPLICA, COLS), bf16),
            pltpu.VMEM((REPLICA, COLS), f32),
            pltpu.VMEM((D, COLS), bf16),
            pltpu.VMEM((D, COLS), bf16),
            pltpu.VMEM((D, COLS), bf16),
            pltpu.VMEM((D, COLS), bf16),
            pltpu.VMEM((REPLICA, COLS), bf16),
            pltpu.VMEM((PIECE, COLS), f32),
            pltpu.VMEM((PIECE, COLS), f32),
            pltpu.VMEM((PIECE, COLS), f32),
            pltpu.VMEM((PIECE, COLS), bf16),
            pltpu.VMEM((PIECE, COLS), bf16),
            pltpu.VMEM((PIECE, COLS), bf16),
            pltpu.VMEM((2, CUTS, 4, SUB, COLS), bf16),
            pltpu.VMEM((2, CUTS, 2, 4, HALF, COLS), bf16),
            pltpu.VMEM((2, CUTS, 2, 4, SUB, COLS), bf16),
            pltpu.VMEM((2, CUTS, 4, SUB, COLS), bf16),
            pltpu.VMEM((2, 16, 8, 128), f32),
            pltpu.VMEM((2, 8, 128), f32),
            pltpu.VMEM((REPLICA, COLS), f32),
            pltpu.SemaphoreType.DMA((N_SEM,)),
            pltpu.SemaphoreType.DMA((N_SEM,)),
            pltpu.SemaphoreType.DMA((5,)),
        ],
        compiler_params=pltpu.CompilerParams(
            collective_id=0, has_side_effects=True, vmem_limit_bytes=56 * 2**20
        ),
    )(patches, cot, master, moment, second)


def solution(mesh):
    in_specs = (
        P(("dp", "shard"), None),
        P("dp", "shard"),
        P("dp", "shard"),
        P("dp", "shard"),
        P("dp", "shard"),
    )
    out_specs = (P(None, "shard"), P("dp", "shard"), P("dp", "shard"), P("dp", "shard"))
    return jax.shard_map(
        on_device, mesh=mesh, in_specs=in_specs, out_specs=out_specs, check_vma=False
    )
```

```python
import jax
import jax.numpy as jnp
from jax import lax
from jax.experimental import pallas as pl
from jax.experimental.pallas import tpu as pltpu
from jax.sharding import PartitionSpec as P

D = 3072
HEAD = 128
QW = 4096
COLS = 256
REPLICA = 2048
BLOCK = 128
PART = 192
PIECE = 768
CUTS = 2
SUB = PART // CUTS
HALF = SUB // 2

MOMENT_FIX = 0.9999734386011124
SECOND_FIX = 0.994079470779666

MESH = pl.DeviceIdType.MESH
f32 = jnp.float32
bf16 = jnp.bfloat16


class Slots:
    def __init__(self):
        self.count = 0

    def take(self, *dims):
        start, size = self.count, 1
        for dim in dims:
            size *= dim
        self.count += size

        def at(*index):
            flat = 0
            for dim, i in zip(dims, index, strict=True):
                flat = flat * dim + i
            return start + flat

        return at


SLOTS = Slots()
Y_SEM = SLOTS.take(2, 2, 4)
YF_SEM = SLOTS.take(2, 2, 4)
Z4_SEM = SLOTS.take(4)
SIB_SEM = SLOTS.take(2, 7)
AG_Z, AG_X, AG_F = SLOTS.take(3, CUTS, 4), SLOTS.take(3, CUTS, 2, 4), SLOTS.take(3, CUTS, 2, 4)
RS_F, RS_X, RS_Z = SLOTS.take(2, CUTS, 2, 4), SLOTS.take(2, CUTS, 2, 4), SLOTS.take(2, CUTS, 4)
SUM_SEM = SLOTS.take(2, 16)
N_SEM = SLOTS.count


def norm_backward(query, centred_cot):
    parts = []
    for head in range(COLS // HEAD):
        lanes = slice(head * HEAD, (head + 1) * HEAD)
        x, c = query[:, lanes], centred_cot[:, lanes]
        x = x - jnp.sum(x, axis=1, keepdims=True) * (1.0 / HEAD)
        var = jnp.sum(x * x, axis=1, keepdims=True) * (1.0 / HEAD)
        rstd = 1.0 / jnp.sqrt(var + 1e-06)
        normed = x * rstd
        inner = jnp.sum(c * normed, axis=1, keepdims=True) * (1.0 / HEAD)
        parts.append((rstd * (c - normed * inner)).astype(bf16))
    return jnp.concatenate(parts, axis=1)


def kernel(
    patches, cot, master_in, moment_in, second_in,
    new_weight, new_master, new_moment, new_second,
    master, moment, second, pat, cots, centred, w0, g1, nw, dq,
    plus, minus, mine, b_two, b_plus, b_minus, b_z, r_f, r_x, r_z, sums, tile, query, lift,
    ssem, rsem, lsem,
):
    dp, sh = lax.axis_index("dp"), lax.axis_index("shard")
    x, zl = dp // 4, dp % 4
    y = (sh // 2) % 4

    def at_x(step):
        return ((x + step) % 4) * 4 + zl, sh

    def at_z(step):
        return x * 4 + (zl + step) % 4, sh

    def at_y(step):
        return dp, (sh // 8) * 8 + ((y + step) % 4) * 2 + sh % 2

    far = (dp, (sh + 8) % 16)
    sibling = (dp, sh + 1 - 2 * (sh % 2))

    def copy(src, dst, slot, to):
        return pltpu.make_async_remote_copy(
            src_ref=src, dst_ref=dst, send_sem=ssem.at[slot], recv_sem=rsem.at[slot],
            device_id=to, device_id_type=MESH,
        )

    started = []

    def send(src, dst, slot, to):
        one = copy(src, dst, slot, to)
        one.start()
        started.append(one)

    def finish():
        for one in started:
            one.wait_send()
        started.clear()

    def arrived(ref, slot):
        copy(ref, ref, slot, sibling).wait_recv()

    def rows(start, size, by):
        return pl.ds(pl.multiple_of(start, by), size)

    barrier = pltpu.get_barrier_semaphore()

    @pl.loop(1, 16)
    def _(p):
        pl.semaphore_signal(barrier, inc=1, device_id=(dp, (sh + p) % 16), device_id_type=MESH)
        pl.semaphore_signal(barrier, inc=1, device_id=((dp + p) % 16, sh), device_id_type=MESH)

    own = pat.at[rows(sh * BLOCK, BLOCK, BLOCK)]
    loads = [
        pltpu.make_async_copy(src, dst, lsem.at[i])
        for i, (src, dst) in enumerate(
            ((master_in, master), (patches, own), (cot, cots), (moment_in, moment), (second_in, second))
        )
    ]
    for load in loads:
        load.start()
    loads[0].wait()
    w0[rows(dp * PART, PART, PART), :] = master[...].astype(bf16)
    loads[1].wait()
    with jax.named_scope("entry"):
        pl.semaphore_wait(barrier, 30)

    def gather_start(k, buf, h):
        part = buf.at[rows(dp * PART + h * SUB, SUB, SUB)]
        for r in (2, 1, 3):
            send(part, part, AG_Z(k, h, r), at_z(r))
        send(part, part, AG_X(k, h, 0, 0), at_x(1))
        send(part, part, AG_X(k, h, 1, 0), at_x(3))

    def gather_z(k, buf, h):
        for r in (1, 3, 2):
            part = buf.at[rows((x * 4 + (zl + 4 - r) % 4) * PART + h * SUB, SUB, SUB)]
            arrived(part, AG_Z(k, h, r))
            send(part, part, AG_X(k, h, 0, r), at_x(1))
            send(part, part, AG_X(k, h, 1, r), at_x(3))

    def gather_x(k, buf, h):
        for r in (0, 1, 3, 2):
            zz = (zl + 4 - r) % 4
            low = ((x + 3) % 4 * 4 + zz) * PART + h * SUB
            arrived(buf.at[rows(low, SUB, SUB)], AG_X(k, h, 0, r))
            half = buf.at[rows(low, HALF, HALF)]
            send(half, half, AG_F(k, h, 0, r), at_x(1))
            high = ((x + 1) % 4 * 4 + zz) * PART + h * SUB
            arrived(buf.at[rows(high, SUB, SUB)], AG_X(k, h, 1, r))
            half = buf.at[rows(high + HALF, HALF, HALF)]
            send(half, half, AG_F(k, h, 1, r), at_x(3))

    def gather_end(k, buf, h):
        for r in (0, 1, 3, 2):
            start = ((x + 2) % 4 * 4 + (zl + 4 - r) % 4) * PART + h * SUB
            arrived(buf.at[rows(start, HALF, HALF)], AG_F(k, h, 0, r))
            arrived(buf.at[rows(start + HALF, HALF, HALF)], AG_F(k, h, 1, r))

    def home(half):
        return (sh + 8 * half) % 16

    def y_block(half, step):
        base = home(half)
        return ((base // 8) * 8 + ((y + step) % 4) * 2 + base % 2) * BLOCK

    def y_send(half, q):
        part = pat.at[rows(home(half) * BLOCK + q * 32, 32, 32)]
        send(part, part, Y_SEM(half, 0, q), at_y(1))
        send(part, part, Y_SEM(half, 1, q), at_y(3))

    def y_forward(half, q):
        low = y_block(half, 3) + q * 32
        arrived(pat.at[rows(low, 32, 32)], Y_SEM(half, 0, q))
        part = pat.at[rows(low, 16, 16)]
        send(part, part, YF_SEM(half, 0, q), at_y(1))
        high = y_block(half, 1) + q * 32
        arrived(pat.at[rows(high, 32, 32)], Y_SEM(half, 1, q))
        part = pat.at[rows(high + 16, 16, 16)]
        send(part, part, YF_SEM(half, 1, q), at_y(3))

    def y_last(half, q):
        start = y_block(half, 2) + q * 32
        arrived(pat.at[rows(start, 16, 16)], YF_SEM(half, 0, q))
        arrived(pat.at[rows(start + 16, 16, 16)], YF_SEM(half, 1, q))
        part = pat.at[rows(start, 32, 32)]
        send(part, part, SIB_SEM(half, 3 + q), sibling)

    def share(half, step, slot):
        part = pat.at[rows(y_block(half, step), BLOCK, BLOCK)]
        send(part, part, SIB_SEM(half, slot), sibling)

    def theirs(half, step):
        return y_block(half, step) // (2 * BLOCK) * (2 * BLOCK) + (1 - sh % 2) * BLOCK

    def shared(half, step, slot):
        arrived(pat.at[rows(theirs(half, step), BLOCK, BLOCK)], SIB_SEM(half, slot))

    def shared_last(half):
        for q in range(4):
            arrived(pat.at[rows(theirs(half, 2) + q * 32, 32, 32)], SIB_SEM(half, 3 + q))

    def block_of(half, step):
        part = rows(y_block(half, step) // (2 * BLOCK) * (2 * BLOCK), 2 * BLOCK, 2 * BLOCK)
        first = jnp.dot(pat[part, :], w0[...], preferred_element_type=f32)
        query[part, :] = first
        dq[part, :] = norm_backward(first, centred[part, :])

    for h in range(CUTS):
        gather_start(0, w0, h)
    for q in range(4):
        y_send(0, q)
    share(0, 0, 0)

    loads[2].wait()

    @pl.loop(0, 8)
    def _(i):
        part = rows(i * 256, 256, 256)
        for head in range(COLS // HEAD):
            lanes = slice(head * HEAD, (head + 1) * HEAD)
            c = cots[part, lanes].astype(f32)
            centred[part, lanes] = c - jnp.sum(c, axis=1, keepdims=True) * (1.0 / HEAD)

    def z4_pass(q):
        arrived(pat.at[rows(home(1) * BLOCK + q * 32, 32, 32)], Z4_SEM(q))
        y_send(1, q)

    y_forward(0, 0)
    for h in range(CUTS):
        gather_z(0, w0, h)
    for q in range(4):
        part = pat.at[rows(sh * BLOCK + q * 32, 32, 32)]
        send(part, part, Z4_SEM(q), far)
    y_forward(0, 1)
    y_forward(0, 2)
    y_forward(0, 3)
    share(0, 3, 1)
    share(0, 1, 2)
    for h in range(CUTS):
        gather_x(0, w0, h)
    z4_pass(0)
    for h in range(CUTS):
        gather_end(0, w0, h)
    shared(0, 0, 0)
    block_of(0, 0)
    shared(0, 3, 1)
    block_of(0, 3)
    shared(0, 1, 2)
    block_of(0, 1)
    for q in range(4):
        y_last(0, q)
    z4_pass(1)
    shared_last(0)
    block_of(0, 2)
    y_forward(1, 0)
    z4_pass(2)
    y_forward(1, 1)
    z4_pass(3)
    share(1, 0, 0)
    y_forward(1, 2)
    shared(1, 0, 0)
    block_of(1, 0)
    y_forward(1, 3)
    share(1, 3, 1)
    share(1, 1, 2)
    for q in range(3):
        y_last(1, q)
    shared(1, 3, 1)
    block_of(1, 3)
    shared(1, 1, 2)
    block_of(1, 1)
    y_last(1, 3)
    shared_last(1)
    block_of(1, 2)

    def piece(step):
        lanes = pl.ds(pl.multiple_of((x + step) % 4 * PIECE, PIECE), PIECE)
        return lax.dot_general(
            pat[:, lanes], dq[...], (((0,), (0,)), ((), ())), preferred_element_type=f32
        )

    ORDER = (2, 1, 3, 0)

    def scatter_two(k, h):
        for r in ORDER:
            start = (zl + r) % 4 * PART + h * SUB
            send(b_two.at[rows(start, HALF, HALF)], r_f.at[k, h, 0, r], RS_F(k, h, 0, r), at_x(1))
            send(b_two.at[rows(start + HALF, HALF, HALF)], r_f.at[k, h, 1, r], RS_F(k, h, 1, r), at_x(3))

    def scatter_x(k, h):
        for r in ORDER:
            start = (zl + r) % 4 * PART + h * SUB
            low, high = rows(start, HALF, HALF), rows(start + HALF, HALF, HALF)
            both = rows(start, SUB, SUB)
            arrived(r_f.at[k, h, 0, r], RS_F(k, h, 0, r))
            b_plus[low, :] = (plus[low, :] + r_f[k, h, 0, r].astype(f32)).astype(bf16)
            b_plus[high, :] = plus[high, :].astype(bf16)
            send(b_plus.at[both], r_x.at[k, h, 0, r], RS_X(k, h, 0, r), at_x(1))
            arrived(r_f.at[k, h, 1, r], RS_F(k, h, 1, r))
            b_minus[low, :] = minus[low, :].astype(bf16)
            b_minus[high, :] = (minus[high, :] + r_f[k, h, 1, r].astype(f32)).astype(bf16)
            send(b_minus.at[both], r_x.at[k, h, 1, r], RS_X(k, h, 1, r), at_x(3))

    def scatter_z(k, h):
        for r in ORDER:
            both = rows((zl + r) % 4 * PART + h * SUB, SUB, SUB)
            arrived(r_x.at[k, h, 0, r], RS_X(k, h, 0, r))
            arrived(r_x.at[k, h, 1, r], RS_X(k, h, 1, r))
            total = mine[both, :] + r_x[k, h, 0, r].astype(f32) + r_x[k, h, 1, r].astype(f32)
            if r:
                b_z[k, h, r] = total.astype(bf16)
                send(b_z.at[k, h, r], r_z.at[k, h, r], RS_Z(k, h, r), at_z(r))
        mine[rows(zl * PART + h * SUB, SUB, SUB), :] = total

    def scatter_end(k, h):
        total = mine[rows(zl * PART + h * SUB, SUB, SUB), :]
        for r in (2, 1, 3):
            arrived(r_z.at[k, h, r], RS_Z(k, h, r))
            total = total + r_z[k, h, r].astype(f32)
        return total

    def scatter_start(k):
        b_two[...] = piece(2).astype(bf16)
        for h in range(CUTS):
            scatter_two(k, h)
        plus[...] = piece(1)
        minus[...] = piece(3)
        scatter_x(k, 0)
        mine[...] = piece(0)
        for h in range(1, CUTS):
            scatter_x(k, h)

    def squares(part):
        part = jnp.sum((part * part).reshape(SUB // 8, 8, COLS), axis=0)
        return part[:, :128] + part[:, 128:]

    scatter_start(0)
    square = None
    for h in range(CUTS):
        scatter_z(0, h)
        if h:
            gather_z(1, g1, h - 1)
        grad1 = scatter_end(0, h)
        g1[rows(dp * PART + h * SUB, SUB, SUB), :] = grad1.astype(bf16)
        gather_start(1, g1, h)
        square = squares(grad1) if square is None else square + squares(grad1)

    tile[0] = square

    def sum_copy(stage, p):
        to = ((dp + p) % 16, sh) if stage == 0 else (dp, (sh + p) % 16)
        return copy(tile.at[stage], sums.at[stage, p], SUM_SEM(stage, p), to)

    def sum_start(stage):
        @pl.loop(1, 16)
        def _(p):
            sum_copy(stage, p).start()

    def sum_end(stage):
        def add(p, total):
            sum_copy(stage, p).wait()
            return total + sums[stage, p]

        return lax.fori_loop(1, 16, add, tile[stage])

    earlier = list(started)
    started.clear()
    sum_start(0)
    for h in range(CUTS - 1):
        gather_x(1, g1, h)
    gather_z(1, g1, CUTS - 1)
    tile[1] = sum_end(0)
    sum_start(1)
    gather_x(1, g1, CUTS - 1)
    for one in earlier:
        one.wait_send()

    def depth(step):
        return (x + step) % 4 * PIECE

    def share_of(part, step):
        span = rows(depth(step), PIECE, PIECE)
        return jnp.dot(pat[part, span], g1[span, :], preferred_element_type=f32)

    @pl.loop(0, 4)
    def _(i):
        part = rows(i * 512, 512, 512)
        lift[part, :] = share_of(part, 0) + share_of(part, 1) + share_of(part, 3)

    for h in range(CUTS):
        gather_end(1, g1, h)
    total = jnp.sum(sum_end(1))
    scale = jnp.sqrt(f32(D * QW)) / jnp.sqrt(total + 1e-12)

    @pl.loop(0, 4)
    def _(i):
        part = rows(i * 512, 512, 512)
        tilted = query[part, :] + scale * (lift[part, :] + share_of(part, 2))
        dq[part, :] = norm_backward(tilted, centred[part, :])

    scatter_start(1)
    for load in loads[3:]:
        load.wait()
    for h in range(CUTS):
        part = pl.ds(h * SUB, SUB)
        scatter_z(1, h)
        if h:
            gather_z(2, nw, h - 1)
        grad2 = scatter_end(1, h)
        weights = master[part, :]
        next_moment = 0.9 * moment[part, :] + 0.1 * grad2
        next_second = 0.95 * second[part, :] + 0.05 * grad2 * grad2
        update = next_moment / MOMENT_FIX / (jnp.sqrt(next_second / SECOND_FIX) + 1e-08) + 0.1 * weights
        next_master = weights - 0.05 * update
        nw[rows(dp * PART + h * SUB, SUB, SUB), :] = next_master.astype(bf16)
        gather_start(2, nw, h)
        new_master[part, :] = next_master
        new_moment[part, :] = next_moment
        new_second[part, :] = next_second
    for h in range(CUTS - 1):
        gather_x(2, nw, h)
    gather_z(2, nw, CUTS - 1)
    gather_x(2, nw, CUTS - 1)

    def place(step):
        part = rows(depth(step), PIECE, PIECE)
        new_weight[part, :] = nw[part, :]

    for step in (0, 1, 3):
        place(step)
    for h in range(CUTS):
        gather_end(2, nw, h)
    place(2)
    finish()


def on_device(patches, cot, master, moment, second):
    state = pltpu.VMEM((PART, COLS), f32)
    any_ref, vmem = pl.BlockSpec(memory_space=pl.ANY), pl.BlockSpec(memory_space=pltpu.VMEM)
    return pl.pallas_call(
        kernel,
        name="sam_step",
        out_shape=(pltpu.VMEM((D, COLS), bf16), state, state, state),
        in_specs=[any_ref] * 5,
        out_specs=(vmem, vmem, vmem, vmem),
        scratch_shapes=[
            pltpu.VMEM((PART, COLS), f32),
            pltpu.VMEM((PART, COLS), f32),
            pltpu.VMEM((PART, COLS), f32),
            pltpu.VMEM((REPLICA, D), bf16),
            pltpu.VMEM((REPLICA, COLS), bf16),
            pltpu.VMEM((REPLICA, COLS), f32),
            pltpu.VMEM((D, COLS), bf16),
            pltpu.VMEM((D, COLS), bf16),
            pltpu.VMEM((D, COLS), bf16),
            pltpu.VMEM((REPLICA, COLS), bf16),
            pltpu.VMEM((PIECE, COLS), f32),
            pltpu.VMEM((PIECE, COLS), f32),
            pltpu.VMEM((PIECE, COLS), f32),
            pltpu.VMEM((PIECE, COLS), bf16),
            pltpu.VMEM((PIECE, COLS), bf16),
            pltpu.VMEM((PIECE, COLS), bf16),
            pltpu.VMEM((2, CUTS, 4, SUB, COLS), bf16),
            pltpu.VMEM((2, CUTS, 2, 4, HALF, COLS), bf16),
            pltpu.VMEM((2, CUTS, 2, 4, SUB, COLS), bf16),
            pltpu.VMEM((2, CUTS, 4, SUB, COLS), bf16),
            pltpu.VMEM((2, 16, 8, 128), f32),
            pltpu.VMEM((2, 8, 128), f32),
            pltpu.VMEM((REPLICA, COLS), f32),
            pltpu.VMEM((REPLICA, COLS), f32),
            pltpu.SemaphoreType.DMA((N_SEM,)),
            pltpu.SemaphoreType.DMA((N_SEM,)),
            pltpu.SemaphoreType.DMA((5,)),
        ],
        compiler_params=pltpu.CompilerParams(
            collective_id=0, has_side_effects=True, vmem_limit_bytes=56 * 2**20
        ),
    )(patches, cot, master, moment, second)


def solution(mesh):
    in_specs = (
        P(("dp", "shard"), None),
        P("dp", "shard"),
        P("dp", "shard"),
        P("dp", "shard"),
        P("dp", "shard"),
    )
    out_specs = (P(None, "shard"), P("dp", "shard"), P("dp", "shard"), P("dp", "shard"))
    return jax.shard_map(
        on_device, mesh=mesh, in_specs=in_specs, out_specs=out_specs, check_vma=False
    )
```

```python
import jax
import jax.numpy as jnp
from jax import lax
from jax.experimental import pallas as pl
from jax.experimental.pallas import tpu as pltpu
from jax.sharding import PartitionSpec as P

D = 3072
HEAD = 128
QW = 4096
COLS = 256
REPLICA = 2048
BLOCK = 128
PART = 192
PIECE = 768
CUTS = 2
SUB = PART // CUTS
HALF = SUB // 2

MOMENT_FIX = 0.9999734386011124
SECOND_FIX = 0.994079470779666

MESH = pl.DeviceIdType.MESH
f32 = jnp.float32
bf16 = jnp.bfloat16


class Slots:
    def __init__(self):
        self.count = 0

    def take(self, *dims):
        start, size = self.count, 1
        for dim in dims:
            size *= dim
        self.count += size

        def at(*index):
            flat = 0
            for dim, i in zip(dims, index, strict=True):
                flat = flat * dim + i
            return start + flat

        return at


SLOTS = Slots()
Y_SEM = SLOTS.take(2, 2, 4)
YF_SEM = SLOTS.take(2, 2, 4)
Z4_SEM = SLOTS.take(4)
SIB_SEM = SLOTS.take(2, 7)
AG_Z, AG_X, AG_F = SLOTS.take(3, CUTS, 4), SLOTS.take(3, CUTS, 2, 4), SLOTS.take(3, CUTS, 2, 4)
RS_F, RS_X, RS_Z = SLOTS.take(2, CUTS, 2, 4), SLOTS.take(2, CUTS, 2, 4), SLOTS.take(2, CUTS, 4)
SUM_SEM = SLOTS.take(2, 16)
N_SEM = SLOTS.count


def norm_backward(query, centred_cot):
    parts = []
    for head in range(COLS // HEAD):
        lanes = slice(head * HEAD, (head + 1) * HEAD)
        x, c = query[:, lanes], centred_cot[:, lanes]
        x = x - jnp.sum(x, axis=1, keepdims=True) * (1.0 / HEAD)
        var = jnp.sum(x * x, axis=1, keepdims=True) * (1.0 / HEAD)
        rstd = 1.0 / jnp.sqrt(var + 1e-06)
        normed = x * rstd
        inner = jnp.sum(c * normed, axis=1, keepdims=True) * (1.0 / HEAD)
        parts.append((rstd * (c - normed * inner)).astype(bf16))
    return jnp.concatenate(parts, axis=1)


def kernel(
    patches, cot, master_in, moment_in, second_in,
    new_weight, new_master, new_moment, new_second,
    master, moment, second, pat, cots, centred, w0, g1, nw, dq,
    two, plus, minus, mine, b_two, b_plus, b_minus, b_z, r_f, r_x, r_z, sums, tile, query, lift,
    ssem, rsem, lsem,
):
    dp, sh = lax.axis_index("dp"), lax.axis_index("shard")
    x, zl = dp // 4, dp % 4
    y = (sh // 2) % 4

    def at_x(step):
        return ((x + step) % 4) * 4 + zl, sh

    def at_z(step):
        return x * 4 + (zl + step) % 4, sh

    def at_y(step):
        return dp, (sh // 8) * 8 + ((y + step) % 4) * 2 + sh % 2

    far = (dp, (sh + 8) % 16)
    sibling = (dp, sh + 1 - 2 * (sh % 2))

    def copy(src, dst, slot, to):
        return pltpu.make_async_remote_copy(
            src_ref=src, dst_ref=dst, send_sem=ssem.at[slot], recv_sem=rsem.at[slot],
            device_id=to, device_id_type=MESH,
        )

    started = []

    def send(src, dst, slot, to):
        one = copy(src, dst, slot, to)
        one.start()
        started.append(one)

    def finish():
        for one in started:
            one.wait_send()
        started.clear()

    def arrived(ref, slot):
        copy(ref, ref, slot, sibling).wait_recv()

    def rows(start, size, by):
        return pl.ds(pl.multiple_of(start, by), size)

    barrier = pltpu.get_barrier_semaphore()

    @pl.loop(1, 16)
    def _(p):
        pl.semaphore_signal(barrier, inc=1, device_id=(dp, (sh + p) % 16), device_id_type=MESH)
        pl.semaphore_signal(barrier, inc=1, device_id=((dp + p) % 16, sh), device_id_type=MESH)

    own = pat.at[rows(sh * BLOCK, BLOCK, BLOCK)]
    loads = [
        pltpu.make_async_copy(src, dst, lsem.at[i])
        for i, (src, dst) in enumerate(
            ((master_in, master), (patches, own), (cot, cots), (moment_in, moment), (second_in, second))
        )
    ]
    for load in loads:
        load.start()
    loads[0].wait()
    w0[rows(dp * PART, PART, PART), :] = master[...].astype(bf16)
    loads[1].wait()
    with jax.named_scope("entry"):
        pl.semaphore_wait(barrier, 30)

    def gather_start(k, buf, h):
        part = buf.at[rows(dp * PART + h * SUB, SUB, SUB)]
        for r in (2, 3, 1):
            send(part, part, AG_Z(k, h, r), at_z(r))
        send(part, part, AG_X(k, h, 0, 0), at_x(1))
        send(part, part, AG_X(k, h, 1, 0), at_x(3))

    def gather_z(k, buf, h):
        for r in (1, 3, 2):
            part = buf.at[rows((x * 4 + (zl + 4 - r) % 4) * PART + h * SUB, SUB, SUB)]
            arrived(part, AG_Z(k, h, r))
            send(part, part, AG_X(k, h, 0, r), at_x(1))
            send(part, part, AG_X(k, h, 1, r), at_x(3))

    def gather_x(k, buf, h):
        for r in (0, 1, 3, 2):
            zz = (zl + 4 - r) % 4
            low = ((x + 3) % 4 * 4 + zz) * PART + h * SUB
            arrived(buf.at[rows(low, SUB, SUB)], AG_X(k, h, 0, r))
            half = buf.at[rows(low, HALF, HALF)]
            send(half, half, AG_F(k, h, 0, r), at_x(1))
            high = ((x + 1) % 4 * 4 + zz) * PART + h * SUB
            arrived(buf.at[rows(high, SUB, SUB)], AG_X(k, h, 1, r))
            half = buf.at[rows(high + HALF, HALF, HALF)]
            send(half, half, AG_F(k, h, 1, r), at_x(3))

    def gather_end(k, buf, h):
        for r in (0, 1, 3, 2):
            start = ((x + 2) % 4 * 4 + (zl + 4 - r) % 4) * PART + h * SUB
            arrived(buf.at[rows(start, HALF, HALF)], AG_F(k, h, 0, r))
            arrived(buf.at[rows(start + HALF, HALF, HALF)], AG_F(k, h, 1, r))

    def home(half):
        return (sh + 8 * half) % 16

    def y_block(half, step):
        base = home(half)
        return ((base // 8) * 8 + ((y + step) % 4) * 2 + base % 2) * BLOCK

    def y_send(half, q):
        part = pat.at[rows(home(half) * BLOCK + q * 32, 32, 32)]
        send(part, part, Y_SEM(half, 0, q), at_y(1))
        send(part, part, Y_SEM(half, 1, q), at_y(3))

    def y_forward(half, q):
        low = y_block(half, 3) + q * 32
        arrived(pat.at[rows(low, 32, 32)], Y_SEM(half, 0, q))
        part = pat.at[rows(low, 16, 16)]
        send(part, part, YF_SEM(half, 0, q), at_y(1))
        high = y_block(half, 1) + q * 32
        arrived(pat.at[rows(high, 32, 32)], Y_SEM(half, 1, q))
        part = pat.at[rows(high + 16, 16, 16)]
        send(part, part, YF_SEM(half, 1, q), at_y(3))

    def y_last(half, q):
        start = y_block(half, 2) + q * 32
        arrived(pat.at[rows(start, 16, 16)], YF_SEM(half, 0, q))
        arrived(pat.at[rows(start + 16, 16, 16)], YF_SEM(half, 1, q))
        part = pat.at[rows(start, 32, 32)]
        send(part, part, SIB_SEM(half, 3 + q), sibling)

    def share(half, step, slot):
        part = pat.at[rows(y_block(half, step), BLOCK, BLOCK)]
        send(part, part, SIB_SEM(half, slot), sibling)

    def theirs(half, step):
        return y_block(half, step) // (2 * BLOCK) * (2 * BLOCK) + (1 - sh % 2) * BLOCK

    def shared(half, step, slot):
        arrived(pat.at[rows(theirs(half, step), BLOCK, BLOCK)], SIB_SEM(half, slot))

    def shared_last(half):
        for q in range(4):
            arrived(pat.at[rows(theirs(half, 2) + q * 32, 32, 32)], SIB_SEM(half, 3 + q))

    def block_of(half, step):
        part = rows(y_block(half, step) // (2 * BLOCK) * (2 * BLOCK), 2 * BLOCK, 2 * BLOCK)
        first = jnp.dot(pat[part, :], w0[...], preferred_element_type=f32)
        query[part, :] = first
        dq[part, :] = norm_backward(first, centred[part, :])

    for h in range(CUTS):
        gather_start(0, w0, h)
    for q in range(4):
        y_send(0, q)
    share(0, 0, 0)

    loads[2].wait()

    @pl.loop(0, 8)
    def _(i):
        part = rows(i * 256, 256, 256)
        for head in range(COLS // HEAD):
            lanes = slice(head * HEAD, (head + 1) * HEAD)
            c = cots[part, lanes].astype(f32)
            centred[part, lanes] = c - jnp.sum(c, axis=1, keepdims=True) * (1.0 / HEAD)

    def piece(step, part):
        lanes = pl.ds(pl.multiple_of((x + step) % 4 * PIECE, PIECE), PIECE)
        return lax.dot_general(
            pat[part, lanes], dq[part, :], (((0,), (0,)), ((), ())), preferred_element_type=f32
        )

    near = rows(sh // 8 * (REPLICA // 2), REPLICA // 2, REPLICA // 2)
    beyond = rows((1 - sh // 8) * (REPLICA // 2), REPLICA // 2, REPLICA // 2)

    def z4_pass(q):
        arrived(pat.at[rows(home(1) * BLOCK + q * 32, 32, 32)], Z4_SEM(q))
        y_send(1, q)

    y_forward(0, 0)
    for h in range(CUTS):
        gather_z(0, w0, h)
    for q in range(4):
        part = pat.at[rows(sh * BLOCK + q * 32, 32, 32)]
        send(part, part, Z4_SEM(q), far)
    y_forward(0, 1)
    y_forward(0, 2)
    y_forward(0, 3)
    share(0, 3, 1)
    share(0, 1, 2)
    for h in range(CUTS):
        gather_x(0, w0, h)
    z4_pass(0)
    for h in range(CUTS):
        gather_end(0, w0, h)
    shared(0, 0, 0)
    block_of(0, 0)
    shared(0, 3, 1)
    block_of(0, 3)
    shared(0, 1, 2)
    block_of(0, 1)
    for q in range(4):
        y_last(0, q)
    z4_pass(1)
    shared_last(0)
    block_of(0, 2)
    y_forward(1, 0)
    two[...] = piece(2, near)
    plus[...] = piece(1, near)
    z4_pass(2)
    y_forward(1, 1)
    minus[...] = piece(3, near)
    mine[...] = piece(0, near)
    z4_pass(3)
    share(1, 0, 0)
    y_forward(1, 2)
    shared(1, 0, 0)
    block_of(1, 0)
    y_forward(1, 3)
    share(1, 3, 1)
    share(1, 1, 2)
    for q in range(3):
        y_last(1, q)
    shared(1, 3, 1)
    block_of(1, 3)
    shared(1, 1, 2)
    block_of(1, 1)
    y_last(1, 3)
    shared_last(1)
    block_of(1, 2)

    ORDER = (2, 1, 3, 0)

    def scatter_two(k, h):
        for r in ORDER:
            start = (zl + r) % 4 * PART + h * SUB
            send(b_two.at[rows(start, HALF, HALF)], r_f.at[k, h, 0, r], RS_F(k, h, 0, r), at_x(1))
            send(b_two.at[rows(start + HALF, HALF, HALF)], r_f.at[k, h, 1, r], RS_F(k, h, 1, r), at_x(3))

    def scatter_x(k, h):
        for r in ORDER:
            start = (zl + r) % 4 * PART + h * SUB
            low, high = rows(start, HALF, HALF), rows(start + HALF, HALF, HALF)
            both = rows(start, SUB, SUB)
            arrived(r_f.at[k, h, 0, r], RS_F(k, h, 0, r))
            b_plus[low, :] = (plus[low, :] + r_f[k, h, 0, r].astype(f32)).astype(bf16)
            b_plus[high, :] = plus[high, :].astype(bf16)
            send(b_plus.at[both], r_x.at[k, h, 0, r], RS_X(k, h, 0, r), at_x(1))
            arrived(r_f.at[k, h, 1, r], RS_F(k, h, 1, r))
            b_minus[low, :] = minus[low, :].astype(bf16)
            b_minus[high, :] = (minus[high, :] + r_f[k, h, 1, r].astype(f32)).astype(bf16)
            send(b_minus.at[both], r_x.at[k, h, 1, r], RS_X(k, h, 1, r), at_x(3))

    def scatter_z(k, h):
        for r in ORDER:
            both = rows((zl + r) % 4 * PART + h * SUB, SUB, SUB)
            arrived(r_x.at[k, h, 0, r], RS_X(k, h, 0, r))
            arrived(r_x.at[k, h, 1, r], RS_X(k, h, 1, r))
            total = mine[both, :] + r_x[k, h, 0, r].astype(f32) + r_x[k, h, 1, r].astype(f32)
            if r:
                b_z[k, h, r] = total.astype(bf16)
                send(b_z.at[k, h, r], r_z.at[k, h, r], RS_Z(k, h, r), at_z(r))
        mine[rows(zl * PART + h * SUB, SUB, SUB), :] = total

    def scatter_end(k, h):
        total = mine[rows(zl * PART + h * SUB, SUB, SUB), :]
        for r in (2, 1, 3):
            arrived(r_z.at[k, h, r], RS_Z(k, h, r))
            total = total + r_z[k, h, r].astype(f32)
        return total

    def scatter_start(k):
        def add(ref, step):
            if k == 0:
                return ref[...] + piece(step, beyond)
            return piece(step, pl.ds(0, REPLICA))

        b_two[...] = add(two, 2).astype(bf16)
        for h in range(CUTS):
            scatter_two(k, h)
        plus[...] = add(plus, 1)
        minus[...] = add(minus, 3)
        scatter_x(k, 0)
        mine[...] = add(mine, 0)
        for h in range(1, CUTS):
            scatter_x(k, h)

    def squares(part):
        part = jnp.sum((part * part).reshape(SUB // 8, 8, COLS), axis=0)
        return part[:, :128] + part[:, 128:]

    scatter_start(0)
    square = None
    for h in range(CUTS):
        scatter_z(0, h)
        if h:
            gather_z(1, g1, h - 1)
        grad1 = scatter_end(0, h)
        g1[rows(dp * PART + h * SUB, SUB, SUB), :] = grad1.astype(bf16)
        gather_start(1, g1, h)
        square = squares(grad1) if square is None else square + squares(grad1)

    tile[0] = square

    def sum_copy(stage, p):
        to = ((dp + p) % 16, sh) if stage == 0 else (dp, (sh + p) % 16)
        return copy(tile.at[stage], sums.at[stage, p], SUM_SEM(stage, p), to)

    def sum_start(stage):
        @pl.loop(1, 16)
        def _(p):
            sum_copy(stage, p).start()

    def sum_end(stage):
        def add(p, total):
            sum_copy(stage, p).wait()
            return total + sums[stage, p]

        return lax.fori_loop(1, 16, add, tile[stage])

    earlier = list(started)
    started.clear()
    sum_start(0)
    for h in range(CUTS - 1):
        gather_x(1, g1, h)
    gather_z(1, g1, CUTS - 1)
    tile[1] = sum_end(0)
    sum_start(1)
    gather_x(1, g1, CUTS - 1)
    for one in earlier:
        one.wait_send()

    def depth(step):
        return (x + step) % 4 * PIECE

    def share_of(part, step):
        span = rows(depth(step), PIECE, PIECE)
        return jnp.dot(pat[part, span], g1[span, :], preferred_element_type=f32)

    @pl.loop(0, 4)
    def _(i):
        part = rows(i * 512, 512, 512)
        lift[part, :] = share_of(part, 0) + share_of(part, 1) + share_of(part, 3)

    for h in range(CUTS):
        gather_end(1, g1, h)
    total = jnp.sum(sum_end(1))
    scale = jnp.sqrt(f32(D * QW)) / jnp.sqrt(total + 1e-12)

    @pl.loop(0, 4)
    def _(i):
        part = rows(i * 512, 512, 512)
        tilted = query[part, :] + scale * (lift[part, :] + share_of(part, 2))
        dq[part, :] = norm_backward(tilted, centred[part, :])

    scatter_start(1)
    for load in loads[3:]:
        load.wait()
    for h in range(CUTS):
        part = pl.ds(h * SUB, SUB)
        scatter_z(1, h)
        if h:
            gather_z(2, nw, h - 1)
        grad2 = scatter_end(1, h)
        weights = master[part, :]
        next_moment = 0.9 * moment[part, :] + 0.1 * grad2
        next_second = 0.95 * second[part, :] + 0.05 * grad2 * grad2
        update = next_moment / MOMENT_FIX / (jnp.sqrt(next_second / SECOND_FIX) + 1e-08) + 0.1 * weights
        next_master = weights - 0.05 * update
        nw[rows(dp * PART + h * SUB, SUB, SUB), :] = next_master.astype(bf16)
        gather_start(2, nw, h)
        new_master[part, :] = next_master
        new_moment[part, :] = next_moment
        new_second[part, :] = next_second
    for h in range(CUTS - 1):
        gather_x(2, nw, h)
    gather_z(2, nw, CUTS - 1)
    gather_x(2, nw, CUTS - 1)

    def place(step):
        part = rows(depth(step), PIECE, PIECE)
        new_weight[part, :] = nw[part, :]

    for step in (0, 1, 3):
        place(step)
    for h in range(CUTS):
        gather_end(2, nw, h)
    place(2)
    finish()


def on_device(patches, cot, master, moment, second):
    state = pltpu.VMEM((PART, COLS), f32)
    any_ref, vmem = pl.BlockSpec(memory_space=pl.ANY), pl.BlockSpec(memory_space=pltpu.VMEM)
    return pl.pallas_call(
        kernel,
        name="sam_step",
        out_shape=(pltpu.VMEM((D, COLS), bf16), state, state, state),
        in_specs=[any_ref] * 5,
        out_specs=(vmem, vmem, vmem, vmem),
        scratch_shapes=[
            pltpu.VMEM((PART, COLS), f32),
            pltpu.VMEM((PART, COLS), f32),
            pltpu.VMEM((PART, COLS), f32),
            pltpu.VMEM((REPLICA, D), bf16),
            pltpu.VMEM((REPLICA, COLS), bf16),
            pltpu.VMEM((REPLICA, COLS), f32),
            pltpu.VMEM((D, COLS), bf16),
            pltpu.VMEM((D, COLS), bf16),
            pltpu.VMEM((D, COLS), bf16),
            pltpu.VMEM((REPLICA, COLS), bf16),
            pltpu.VMEM((PIECE, COLS), f32),
            pltpu.VMEM((PIECE, COLS), f32),
            pltpu.VMEM((PIECE, COLS), f32),
            pltpu.VMEM((PIECE, COLS), f32),
            pltpu.VMEM((PIECE, COLS), bf16),
            pltpu.VMEM((PIECE, COLS), bf16),
            pltpu.VMEM((PIECE, COLS), bf16),
            pltpu.VMEM((2, CUTS, 4, SUB, COLS), bf16),
            pltpu.VMEM((2, CUTS, 2, 4, HALF, COLS), bf16),
            pltpu.VMEM((2, CUTS, 2, 4, SUB, COLS), bf16),
            pltpu.VMEM((2, CUTS, 4, SUB, COLS), bf16),
            pltpu.VMEM((2, 16, 8, 128), f32),
            pltpu.VMEM((2, 8, 128), f32),
            pltpu.VMEM((REPLICA, COLS), f32),
            pltpu.VMEM((REPLICA, COLS), f32),
            pltpu.SemaphoreType.DMA((N_SEM,)),
            pltpu.SemaphoreType.DMA((N_SEM,)),
            pltpu.SemaphoreType.DMA((5,)),
        ],
        compiler_params=pltpu.CompilerParams(
            collective_id=0, has_side_effects=True, vmem_limit_bytes=56 * 2**20
        ),
    )(patches, cot, master, moment, second)


def solution(mesh):
    in_specs = (
        P(("dp", "shard"), None),
        P("dp", "shard"),
        P("dp", "shard"),
        P("dp", "shard"),
        P("dp", "shard"),
    )
    out_specs = (P(None, "shard"), P("dp", "shard"), P("dp", "shard"), P("dp", "shard"))
    return jax.shard_map(
        on_device, mesh=mesh, in_specs=in_specs, out_specs=out_specs, check_vma=False
    )
```
